32 devices in a mesh: row: 8 (over z, y), col: 4 (over x, core).
Axes of the slice: x: 2, y: 2, z: 4, core: 2. Of those that a mesh axis runs over, the one named last changes fastest.
Arguments:
- couple_features: bfloat16 [256, 256, 128], P('row', 'col'), may hold values from -6 to 6
- homolog_features: bfloat16 [48, 256, 64], P('col', 'row'), may hold values from -6 to 6
- genuine_position_flags: int32 [256], P('row'), may hold values from 0 to 1, as said below
- homolog_availability: int32 [48], P('col'), may hold values from 0 to 1, as said below
- primary_factor_matrix: bfloat16 [64, 32], replicated, may hold values from -0.75 to 0.75
- secondary_factor_matrix: bfloat16 [64, 32], replicated, may hold values from -0.75 to 0.75
- contraction_matrix: bfloat16 [1024, 128], replicated, may hold values from -0.1875 to 0.1875
- contraction_offset: float32 [128], replicated, may hold values from -3 to 3
- attention_score_matrix: bfloat16 [128, 8], replicated, may hold values from -100 to 100
- content_projection_matrix: bfloat16 [64, 256], replicated, may hold values from -0.75 to 0.75
- sigmoid_switch_matrix: bfloat16 [64, 256], replicated, may hold values from -0.75 to 0.75
- final_projection_matrix: bfloat16 [256, 64], replicated, may hold values from -0.375 to 0.375
Outputs:
- pair_output: bfloat16 [256, 256, 128], P('row', 'col')
- refreshed_homologs: bfloat16 [48, 256, 64], P('col', 'row')
The draws below stay inside these ranges and needn't reach their ends.
Inputs may be any that keep to these rules, and one draw needn't show every extreme that they name: `genuine_position_flags`: entry 0 is 1 and the last entry is 0. `homolog_availability`: entry 0 is 1 and the last entry is 0.
All inputs are finite; a program needn't handle non-finite values.
Results may differ from the reference program's by a relative error of at most 0.0093.
Values may be sent and summed in bfloat16 or wider, within the bound.
A program may use at most 64 MiB of HBM per device.

```python
import math
import jax
import jax.numpy as jnp
from jax import lax

FEATURE_DEPTH = 64
C_Z = 128
FACTOR_WIDTH = 32
ATTENTION_HEADS = 8
PER_HEAD_WIDTH = 32
HOMOLOG_NUMBER = 48
CHAIN_LENGTH = 256


def draw_genuine_position_flags(key, part):
    levels = jax.random.randint(key, (CHAIN_LENGTH,), 0, 8)
    marks = (levels < 7).astype(jnp.int32)
    return marks.at[0].set(1).at[CHAIN_LENGTH - 1].set(0)


def draw_homolog_availability(key, part):
    levels = jax.random.randint(key, (HOMOLOG_NUMBER,), 0, 4)
    marks = (levels < 3).astype(jnp.int32)
    return marks.at[0].set(1).at[HOMOLOG_NUMBER - 1].set(0)


def draw_attention_score_matrix(key, part):
    key = jax.random.fold_in(key, 7)
    first_key, second_key, third_key = jax.random.split(key, 3)
    base = jax.random.normal(first_key, (C_Z, ATTENTION_HEADS), jnp.float32)
    strong_head = jax.random.randint(third_key, (), 0, ATTENTION_HEADS)
    head_ids = jnp.arange(ATTENTION_HEADS)[None, :]
    head_scale = jnp.exp(jax.random.uniform(second_key, (1, ATTENTION_HEADS), jnp.float32, math.log(0.5), math.log(4.0)))
    head_scale = jnp.where(head_ids == strong_head, 80.0, head_scale)
    return jnp.clip(base * head_scale * C_Z ** (-0.5), -100.0, 100.0).astype(jnp.bfloat16)


def steps_of(key, shape, cuts, low, high):
    gain, own = 1.0, jax.random.fold_in(key, 6)
    for axis_at, parts in cuts:
        heights = jnp.exp(jax.random.uniform(jax.random.fold_in(own, axis_at), (parts,), jnp.float32, low / len(cuts), high / len(cuts)))
        gain = gain * jnp.repeat(heights, shape[axis_at] // parts).reshape([-1 if axis == axis_at else 1 for axis in range(len(shape))])
    return gain


def centred(own_key, extent, deviation, most, pieces=(), kind=jnp.bfloat16):
    array = deviation * jax.random.normal(own_key, extent, jnp.float32)
    if pieces:
        array = array * steps_of(own_key, extent, pieces, -0.22, 0.18)
    return jnp.clip(array, -most, most).astype(kind)


def setup_inputs(seed: int = 0) -> dict:
    key_list = jax.random.split(jax.random.key(seed), 13)
    couple_features = centred(key_list[0], (CHAIN_LENGTH, CHAIN_LENGTH, C_Z), 1.0, 6.0, ((0, 8), (1, 4)))
    homolog_features = centred(key_list[1], (HOMOLOG_NUMBER, CHAIN_LENGTH, FEATURE_DEPTH), 1.0, 6.0, ((0, 4), (1, 8)))
    genuine_position_flags = draw_genuine_position_flags(jax.random.fold_in(key_list[12], 71), 0)
    homolog_availability = draw_homolog_availability(jax.random.fold_in(key_list[12], 71), 0)
    primary_factor_matrix = centred(key_list[4], (FEATURE_DEPTH, FACTOR_WIDTH), FEATURE_DEPTH ** -0.5, 0.75)
    secondary_factor_matrix = centred(key_list[5], (FEATURE_DEPTH, FACTOR_WIDTH), FEATURE_DEPTH ** -0.5, 0.75)
    contraction_matrix = centred(key_list[6], (FACTOR_WIDTH * FACTOR_WIDTH, C_Z), (FACTOR_WIDTH * FACTOR_WIDTH) ** -0.5, 0.1875)
    contraction_offset = centred(key_list[7], (C_Z,), 0.5, 3.0, (), jnp.float32)
    attention_score_matrix = draw_attention_score_matrix(jax.random.fold_in(key_list[12], 71), 0)
    content_projection_matrix = centred(key_list[9], (FEATURE_DEPTH, ATTENTION_HEADS * PER_HEAD_WIDTH), FEATURE_DEPTH ** -0.5, 0.75)
    sigmoid_switch_matrix = centred(key_list[10], (FEATURE_DEPTH, ATTENTION_HEADS * PER_HEAD_WIDTH), FEATURE_DEPTH ** -0.5, 0.75)
    final_projection_matrix = centred(key_list[11], (ATTENTION_HEADS * PER_HEAD_WIDTH, FEATURE_DEPTH), (ATTENTION_HEADS * PER_HEAD_WIDTH) ** -0.5, 0.375)
    return {"couple_features": couple_features, "homolog_features": homolog_features, "genuine_position_flags": genuine_position_flags, "homolog_availability": homolog_availability, "primary_factor_matrix": primary_factor_matrix, "secondary_factor_matrix": secondary_factor_matrix, "contraction_matrix": contraction_matrix, "contraction_offset": contraction_offset, "attention_score_matrix": attention_score_matrix, "content_projection_matrix": content_projection_matrix, "sigmoid_switch_matrix": sigmoid_switch_matrix, "final_projection_matrix": final_projection_matrix}


EPSILON = 1e-05

def standardize_features(inputs):
    mean_value = lax.optimization_barrier(jnp.mean(inputs, axis=-1, keepdims=True))
    centered = inputs - mean_value
    variance = lax.optimization_barrier(jnp.mean(centered * centered, axis=-1, keepdims=True))
    return centered * lax.rsqrt(variance + EPSILON)

def reference(couple_features, homolog_features, genuine_position_flags, homolog_availability, primary_factor_matrix, secondary_factor_matrix, contraction_matrix, contraction_offset, attention_score_matrix, content_projection_matrix, sigmoid_switch_matrix, final_projection_matrix):
    sequence_mask_float = homolog_availability.astype(jnp.float32)
    tok_float = genuine_position_flags.astype(jnp.float32)
    standardized_features = standardize_features(homolog_features.astype(jnp.float32)).astype(jnp.bfloat16)
    left_projected = (jnp.dot(standardized_features, primary_factor_matrix, preferred_element_type=jnp.float32) * sequence_mask_float[:, None, None]).astype(jnp.bfloat16)
    right_projected = (jnp.dot(standardized_features, secondary_factor_matrix, preferred_element_type=jnp.float32) * sequence_mask_float[:, None, None]).astype(jnp.bfloat16)
    seq_count = jnp.sum(sequence_mask_float)
    value_rows_gathered = jnp.dot(standardized_features, content_projection_matrix, preferred_element_type=jnp.float32).astype(jnp.bfloat16)
    values_heads = value_rows_gathered.reshape(HOMOLOG_NUMBER, CHAIN_LENGTH, ATTENTION_HEADS, PER_HEAD_WIDTH).astype(jnp.float32)
    block_rows = math.gcd(CHAIN_LENGTH, 32)
    blocks = CHAIN_LENGTH // block_rows
    left_blocks = left_projected.reshape(HOMOLOG_NUMBER, blocks, block_rows, FACTOR_WIDTH).transpose(1, 0, 2, 3)
    pair_blocks = couple_features.reshape(blocks, block_rows, CHAIN_LENGTH, C_Z)
    tok_blocks = tok_float.reshape(blocks, block_rows)
    right_float = right_projected.astype(jnp.float32)
    col_bias = (tok_float - 1.0) * 1000000000.0

    def row_block(inputs):
        left_block, pair_block, tok_block = inputs
        outer = jnp.einsum('sic,sjd->ijcd', left_block.astype(jnp.float32), right_float)
        outer = outer.astype(jnp.bfloat16).reshape(block_rows * CHAIN_LENGTH, FACTOR_WIDTH * FACTOR_WIDTH)
        update = jnp.dot(outer, contraction_matrix, preferred_element_type=jnp.float32).reshape(block_rows, CHAIN_LENGTH, C_Z) / seq_count + contraction_offset
        pair_new = (pair_block.astype(jnp.float32) + tok_block[:, None, None] * tok_float[None, :, None] * update).astype(jnp.bfloat16)
        pair_norm = standardize_features(pair_new.astype(jnp.float32)).astype(jnp.bfloat16)
        logits = jnp.dot(pair_norm, attention_score_matrix, preferred_element_type=jnp.float32) + col_bias[None, :, None]
        row_top = lax.optimization_barrier(jnp.max(logits, axis=1, keepdims=True))
        expd = jnp.exp(logits - row_top)
        weights = (expd / lax.optimization_barrier(jnp.sum(expd, axis=1, keepdims=True))).astype(jnp.bfloat16)
        averaged = jnp.einsum('ijh,sjhc->sihc', weights.astype(jnp.float32), values_heads)
        return (pair_new, averaged)
    pair_parts, avg_parts = lax.map(row_block, (left_blocks, pair_blocks, tok_blocks))
    pair_output = pair_parts.reshape(CHAIN_LENGTH, CHAIN_LENGTH, C_Z)
    averaged = avg_parts.transpose(1, 0, 2, 3, 4).reshape(HOMOLOG_NUMBER, CHAIN_LENGTH, ATTENTION_HEADS * PER_HEAD_WIDTH)
    gate_values = jax.nn.sigmoid(jnp.dot(standardized_features, sigmoid_switch_matrix, preferred_element_type=jnp.float32))
    switched_result = (gate_values * averaged).astype(jnp.bfloat16)
    refreshed_homologs = (homolog_features.astype(jnp.float32) + jnp.dot(switched_result, final_projection_matrix, preferred_element_type=jnp.float32)).astype(jnp.bfloat16)
    return (pair_output, refreshed_homologs)
```

```python
import functools

import jax
import jax.numpy as jnp
from jax import lax
from jax.experimental import pallas as pl
from jax.experimental.pallas import tpu as pltpu
from jax.sharding import PartitionSpec as P

EPSILON = 1e-05
MESH = pl.DeviceIdType.MESH
BF16 = jnp.bfloat16
F32 = jnp.float32


def standardize(inputs):
    mean_value = jnp.mean(inputs, axis=-1, keepdims=True)
    centered = inputs - mean_value
    variance = jnp.mean(centered * centered, axis=-1, keepdims=True)
    return centered * lax.rsqrt(variance + EPSILON)


def kernel(
    R, C, S,
    couple, hom, norm, lblk, rblk, flags, w_dcz, offset, score, content, switch, final,
    pair_out, hom_out,
    lbuf, rbuf, nbuf, lgbuf, wbd, pbuf, ubuf, vbuf, gbuf, wtmp, mcol,
    lsend, lrecv, rsend, rrecv, nsend, nrecv, gsend, grecv,
):
    I, J, Z = couple.shape
    F = w_dcz.shape[0]
    H = score.shape[1]
    S2 = norm.shape[0]
    CH = norm.shape[2] // 2
    HC = content.shape[1]
    HV = J // I
    SP = lblk.shape[0]
    PK = Z // F
    IG = I // PK
    r = lax.axis_index("row")
    c = lax.axis_index("col")
    target = lax.div(r, HV)
    part = lax.rem(r, HV)
    own_target = target == c

    barrier = pltpu.get_barrier_semaphore()

    def greet(row, col):
        pl.semaphore_signal(barrier, inc=1, device_id=(row, col), device_id_type=MESH)

    for k in range(1, C):
        greet(r, lax.rem(c + k, C))
    for k in range(1, R):
        greet(lax.rem(r + k, R), c)
    for half in range(HV):
        for k in range(C):
            row, col = c * HV + half, lax.rem(c + k, C)
            if k == 0:
                pl.when(jnp.logical_not(row == r))(functools.partial(greet, row, col))
            else:
                greet(row, col)

    wbd[...] = jnp.zeros_like(wbd)
    for d in range(F):
        block = w_dcz[d]
        for p in range(PK):
            wbd[pl.ds(d * Z + p * F, F), pl.ds(p * Z, Z)] = block

    pl.semaphore_wait(barrier, (C - 1) + (R - 1) + R - own_target.astype(jnp.int32))

    def right_copy(k, row):
        return pltpu.make_async_remote_copy(
            src_ref=rblk, dst_ref=rbuf.at[part, c], send_sem=rsend.at[k],
            recv_sem=rrecv.at[part, c], device_id=(row, target), device_id_type=MESH)

    for k in range(1, R):
        right_copy(k, lax.rem(r + k, R)).start()

    @pl.when(jnp.logical_not(own_target))
    def _():
        right_copy(0, r).start()

    left_copies = []
    for k in range(1, C):
        copy = pltpu.make_async_remote_copy(
            src_ref=lblk, dst_ref=lbuf.at[c], send_sem=lsend.at[k],
            recv_sem=lrecv.at[c], device_id=(r, lax.rem(c + k, C)), device_id_type=MESH)
        copy.start()
        left_copies.append(copy)

    norm_copies = []
    for k in range(1, R):
        copy = pltpu.make_async_remote_copy(
            src_ref=norm, dst_ref=nbuf.at[r], send_sem=nsend.at[k],
            recv_sem=nrecv.at[r], device_id=(lax.rem(r + k, R), c), device_id_type=MESH)
        copy.start()
        norm_copies.append(copy)

    lbuf[c] = lblk[...]
    nbuf[r] = norm[...]

    @pl.when(own_target)
    def _():
        rbuf[part, c] = rblk[...]

    zero = jnp.zeros((CH, HC), BF16)

    def doubled(m):
        return jnp.concatenate(
            [jnp.concatenate([m, zero], axis=1), jnp.concatenate([zero, m], axis=1)], axis=0)

    switch2 = doubled(switch[...])
    for s in range(S2):
        gate = jnp.dot(norm[s], switch2, preferred_element_type=F32)
        gbuf[s] = 1.0 / (1.0 + jnp.exp(-gate))

    for k in range(1, C):
        peer = lax.rem(c + k, C)
        pltpu.make_async_remote_copy(
            src_ref=lblk, dst_ref=lbuf.at[peer], send_sem=lsend.at[k],
            recv_sem=lrecv.at[peer], device_id=(r, peer), device_id_type=MESH).wait_recv()
    for half in range(HV):
        for k in range(C):
            row, col = c * HV + half, lax.rem(c + k, C)

            def arrive(half=half, row=row, col=col, k=k):
                pltpu.make_async_remote_copy(
                    src_ref=rblk, dst_ref=rbuf.at[half, col], send_sem=rsend.at[k],
                    recv_sem=rrecv.at[half, col], device_id=(row, col),
                    device_id_type=MESH).wait_recv()

            if k == 0:
                pl.when(jnp.logical_not(row == r))(arrive)
            else:
                arrive()

    count = jnp.zeros((1, 1), F32)
    for k in range(C):
        count = count + lbuf[k][S + 1:S + 2, 0:1].astype(F32)
    inv = 1.0 / count
    left = lbuf[...].reshape(C * SP, I * F)
    step = Z // I
    for half in range(HV):
        def outer(t, carry, half=half):
            at = pl.multiple_of(t * Z, Z)
            lhs = rbuf[half, :, :, pl.ds(at, Z)].reshape(C * SP, Z)
            o = lax.dot_general(lhs, left, (((0,), (0,)), ((), ())),
                                preferred_element_type=F32).astype(BF16)
            for q in range(step):
                for g in range(IG):
                    pbuf[t, pl.ds(g * J + half * I, I), pl.ds(q * Z, Z)] = (
                        o[q * I:(q + 1) * I, g * Z:(g + 1) * Z])
            return carry
        lax.fori_loop(0, F // step, outer, 0)

    ubuf[...] = jnp.zeros_like(ubuf)

    def contract(t, carry):
        at = pl.multiple_of(t * (step * Z), step * Z)
        ubuf[...] += jnp.dot(pbuf[t], wbd[pl.ds(at, step * Z), :], preferred_element_type=F32)
        return carry
    lax.fori_loop(0, F // step, contract, 0)

    rows_of, lanes_of = (lax.broadcasted_iota(jnp.int32, (I, I), n) for n in (0, 1))
    lane_parts = []
    for half in range(HV):
        lane = rbuf[half, 0][S:S + 1, 0:I].astype(F32)
        lane_parts.append(lane)
        spread = jnp.where(rows_of == lanes_of, jnp.broadcast_to(lane, (I, I)), 0.0)
        mcol[pl.ds(half * I, I), :] = jnp.broadcast_to(
            jnp.sum(spread, axis=1, keepdims=True), (I, Z))
    bias = (jnp.concatenate(lane_parts * 2, axis=1) - 1.0) * 1000000000.0

    off = offset[...]
    score_t = score[...].astype(F32).T.astype(BF16)
    hi = I // 2
    own = lgbuf.at[c]

    def epilogue(g, carry):
        for p in range(PK):
            pieces = []
            for upper in range(2):
                i = g * PK + p + upper * hi
                row = pl.multiple_of((g + upper * (IG // 2)) * J, J)
                update = ubuf[pl.ds(row, J), p * Z:(p + 1) * Z] * inv + off
                mark = flags[i].astype(F32)
                new = (couple[i].astype(F32) + (mcol[...] * mark) * update).astype(BF16)
                pair_out[i] = new
                normed = standardize(new.astype(F32)).astype(BF16)
                pieces.append(lax.dot_general(
                    score_t, normed, (((1,), (1,)), ((), ())), preferred_element_type=F32))
            own[g * PK + p] = jnp.concatenate(pieces, axis=1) + bias
        return carry
    lax.fori_loop(0, IG // 2, epilogue, 0)

    logit_copies = []
    for k in range(1, C):
        copy = pltpu.make_async_remote_copy(
            src_ref=lgbuf.at[c], dst_ref=lgbuf.at[c], send_sem=gsend.at[k],
            recv_sem=grecv.at[c], device_id=(r, lax.rem(c + k, C)), device_id_type=MESH)
        copy.start()
        logit_copies.append(copy)

    for k in range(1, R):
        peer = lax.rem(r + k, R)
        pltpu.make_async_remote_copy(
            src_ref=norm, dst_ref=nbuf.at[peer], send_sem=nsend.at[k],
            recv_sem=nrecv.at[peer], device_id=(peer, c), device_id_type=MESH).wait_recv()
    content2 = doubled(content[...])

    def value(s, carry):
        x = nbuf[:, s].reshape(R * I, 2 * CH)
        vbuf[s] = jnp.dot(x, content2, preferred_element_type=F32).astype(BF16)
        return carry
    lax.fori_loop(0, S2, value, 0)

    for k in range(1, C):
        peer = lax.rem(c + k, C)
        pltpu.make_async_remote_copy(
            src_ref=lgbuf.at[peer], dst_ref=lgbuf.at[peer], send_sem=gsend.at[k],
            recv_sem=grecv.at[peer], device_id=(r, peer), device_id_type=MESH).wait_recv()

    for upper in range(2):
        logits = jnp.concatenate(
            [lgbuf[k].reshape(hi * H, 2 * J)[:, upper * J:(upper + 1) * J] for k in range(C)],
            axis=1)
        e = jnp.exp(logits - jnp.max(logits, axis=1, keepdims=True))
        wts = e / jnp.sum(e, axis=1, keepdims=True)
        for at in range(0, C * J, 128):
            wtmp[at // 128, pl.ds(upper * hi * H, hi * H), :] = wts[:, at:at + 128]
    weights = jnp.concatenate(
        [jnp.concatenate([wtmp[a, pl.ds(h, I, stride=H), :] for a in range(C * J // 128)], axis=1)
         for h in range(H)], axis=0).astype(BF16)

    head_lane = lax.rem(lax.broadcasted_iota(jnp.int32, (I, 2 * HC), 1), HC) // (HC // H)
    fin = final[...]

    for s in range(S2):
        full = jnp.dot(weights, vbuf[s], preferred_element_type=F32)
        acc = jnp.zeros((I, 2 * HC), F32)
        for h in range(H):
            acc = jnp.where(head_lane == h, full[h * I:(h + 1) * I], acc)
        gated = (gbuf[s] * acc).astype(BF16)
        for t in range(2):
            seq = s + t * S2
            if seq < S:
                res = jnp.dot(gated[:, t * HC:(t + 1) * HC], fin, preferred_element_type=F32)
                hom_out[seq] = (hom[seq].astype(F32) + res).astype(BF16)

    for k in range(1, R):
        right_copy(k, lax.rem(r + k, R)).wait_send()

    @pl.when(jnp.logical_not(own_target))
    def _():
        right_copy(0, r).wait_send()
    for copy in left_copies + norm_copies + logit_copies:
        copy.wait_send()


def solution(mesh):
    R, C = mesh.shape["row"], mesh.shape["col"]

    def body(couple, hom, flags, avail, w_left, w_right, w_con, offset, score, content, switch,
             final):
        S, I, CH = hom.shape
        J, Z = couple.shape[1:]
        F = w_left.shape[1]
        H = score.shape[1]
        HC = content.shape[1]
        S2 = (S + 1) // 2
        SP = -(-(S + 2) // 16) * 16
        norm = standardize(hom.astype(F32)).astype(BF16)
        marks = avail.astype(F32)
        left = (jnp.dot(norm, w_left, preferred_element_type=F32)
                * marks[:, None, None]).astype(BF16).reshape(S, I * F)
        right = (jnp.dot(norm, w_right, preferred_element_type=F32)
                 * marks[:, None, None]).astype(BF16).transpose(0, 2, 1).reshape(S, F * I)
        count = jnp.broadcast_to(jnp.sum(marks).astype(BF16), (1, I * F))
        pad = lambda n: jnp.zeros((n, I * F), BF16)
        lblk = jnp.concatenate([left, pad(1), count, pad(SP - S - 2)], axis=0)
        tok = jnp.tile(flags.astype(BF16), F)[None]
        rblk = jnp.concatenate([right, tok, pad(SP - S - 1)], axis=0)
        padded = jnp.pad(norm, ((0, 2 * S2 - S), (0, 0), (0, 0)))
        packed = jnp.concatenate([padded[:S2], padded[S2:]], axis=-1)
        w_dcz = w_con.reshape(F, F, Z).transpose(1, 0, 2)
        step = Z // I
        vmem = pl.BlockSpec(memory_space=pltpu.VMEM)
        smem = pl.BlockSpec(memory_space=pltpu.SMEM)
        dma = pltpu.SemaphoreType.DMA
        return pl.pallas_call(
            functools.partial(kernel, R, C, S),
            out_shape=(jax.ShapeDtypeStruct(couple.shape, BF16),
                       jax.ShapeDtypeStruct(hom.shape, BF16)),
            in_specs=[vmem] * 5 + [smem] + [vmem] * 6,
            out_specs=(vmem, vmem),
            scratch_shapes=[
                pltpu.VMEM((C, SP, I * F), BF16),
                pltpu.VMEM((J // I, C, SP, F * I), BF16),
                pltpu.VMEM((R, S2, I, 2 * CH), BF16),
                pltpu.VMEM((C, I // 2, H, 2 * J), F32),
                pltpu.VMEM((F * Z, Z // F * Z), BF16),
                pltpu.VMEM((F // step, I * F // Z * J, step * Z), BF16),
                pltpu.VMEM((I * F // Z * J, Z // F * Z), F32),
                pltpu.VMEM((S2, R * I, 2 * HC), BF16),
                pltpu.VMEM((S2, I, 2 * HC), F32),
                pltpu.VMEM((C * J // 128, I * H, 128), F32),
                pltpu.VMEM((J, Z), F32),
                dma((C,)), dma((C,)), dma((R,)), dma((J // I, C)),
                dma((R,)), dma((R,)), dma((C,)), dma((C,)),
            ],
            compiler_params=pltpu.CompilerParams(
                collective_id=0, has_side_effects=True, vmem_limit_bytes=56 * 2**20),
        )(couple, hom, packed, lblk, rblk, flags, w_dcz, offset.reshape(1, Z), score, content,
          switch, final)

    placed = (P("row", "col", None), P("col", "row", None), P("row"), P("col")) + (P(),) * 8
    return jax.shard_map(
        body, mesh=mesh, in_specs=placed,
        out_specs=(P("row", "col", None), P("col", "row", None)), check_vma=False)
```

```python
import functools

import jax
import jax.numpy as jnp
from jax import lax
from jax.experimental import pallas as pl
from jax.experimental.pallas import tpu as pltpu
from jax.sharding import PartitionSpec as P

EPSILON = 1e-05
MESH = pl.DeviceIdType.MESH
BF16 = jnp.bfloat16
F32 = jnp.float32


def standardize(inputs):
    mean_value = jnp.mean(inputs, axis=-1, keepdims=True)
    centered = inputs - mean_value
    variance = jnp.mean(centered * centered, axis=-1, keepdims=True)
    return centered * lax.rsqrt(variance + EPSILON)


def kernel(
    R, C, S,
    couple, hom, flags, flag_row, avail, w_left, w_right, w_con, offset, score, content, switch,
    final, pair_out, hom_out,
    norm, lblk, rblk, wcon, gated, lbuf, rbuf, nbuf, lgbuf, wbd, pbuf, ubuf, vbuf, gbuf, wtmp, mcol,
    lsend, lrecv, rsend, rrecv, nsend, nrecv, gsend, grecv,
):
    I, J, Z = couple.shape
    F = w_left.shape[0]
    H = score.shape[0]
    S2 = norm.shape[0]
    CH = norm.shape[2] // 2
    HC = content.shape[1]
    HV = J // I
    SP = lblk.shape[0]
    PK = Z // F
    IG = I // PK
    r = lax.axis_index("row")
    c = lax.axis_index("col")
    target = lax.div(r, HV)
    part = lax.rem(r, HV)
    own_target = target == c

    barrier = pltpu.get_barrier_semaphore()

    def greet(row, col):
        pl.semaphore_signal(barrier, inc=1, device_id=(row, col), device_id_type=MESH)

    for k in range(1, C):
        greet(r, lax.rem(c + k, C))
    for k in range(1, R):
        greet(lax.rem(r + k, R), c)
    for half in range(HV):
        for k in range(C):
            row, col = c * HV + half, lax.rem(c + k, C)
            if k == 0:
                pl.when(jnp.logical_not(row == r))(functools.partial(greet, row, col))
            else:
                greet(row, col)

    normed = standardize(hom[...].reshape(S * I, CH).astype(F32)).astype(BF16)
    if S % 2:
        padded = jnp.concatenate([normed, jnp.zeros((I, CH), BF16)], axis=0)
    else:
        padded = normed
    norm[...] = jnp.concatenate(
        [padded[:S2 * I], padded[S2 * I:]], axis=1).reshape(S2, I, 2 * CH)
    feat, lane = (lax.broadcasted_iota(jnp.int32, (F, I * F), n) for n in (0, 1))
    low_f = (lax.rem(lane, F) == feat).astype(F32).astype(BF16)
    high_f = (lax.div(lane, I) == feat).astype(F32).astype(BF16)
    res, lane = (lax.broadcasted_iota(jnp.int32, (I, I * F), n) for n in (0, 1))
    high_i = (lax.div(lane, F) == res).astype(F32)
    low_i = (lax.rem(lane, I) == res).astype(F32)
    seq, lane = (lax.broadcasted_iota(jnp.int32, (SP, S * I), n) for n in (0, 1))
    mark = jnp.zeros((SP, S * I), F32)
    count = jnp.int32(0)
    for n in range(S):
        mark = jnp.where(seq == n, avail[n].astype(F32), mark)
        count = count + avail[n]
    pick = jnp.where(lax.div(lane, I) == seq, mark, 0.0).astype(BF16)
    rows = lax.broadcasted_iota(jnp.int32, (SP, I * F), 0)

    def factors(weight, spread, keep):
        wide = lax.dot_general(weight[...], spread, (((0,), (0,)), ((), ())),
                               preferred_element_type=F32).astype(BF16)
        every = jnp.dot(normed, wide, preferred_element_type=F32).reshape(S, I, I * F)
        own = (every * keep[None]).astype(BF16).reshape(S * I, I * F)
        return jnp.dot(pick, own, preferred_element_type=F32)

    right = factors(w_right, high_f, low_i)
    tok = jnp.dot(jnp.broadcast_to(flag_row[...].astype(F32), (SP, I)).astype(BF16),
                  low_i.astype(BF16), preferred_element_type=F32)
    rblk[...] = jnp.where(rows == S, tok, right).astype(BF16)
    left = factors(w_left, low_f, high_i)
    lblk[...] = jnp.where(rows == S + 1, count.astype(F32), left).astype(BF16)

    pl.semaphore_wait(barrier, (C - 1) + (R - 1) + R - own_target.astype(jnp.int32))

    def right_copy(k, row):
        return pltpu.make_async_remote_copy(
            src_ref=rblk, dst_ref=rbuf.at[part, c], send_sem=rsend.at[k],
            recv_sem=rrecv.at[part, c], device_id=(row, target), device_id_type=MESH)

    for k in range(1, R):
        right_copy(k, lax.rem(r + k, R)).start()

    @pl.when(jnp.logical_not(own_target))
    def _():
        right_copy(0, r).start()

    left_copies = []
    for k in range(1, C):
        copy = pltpu.make_async_remote_copy(
            src_ref=lblk, dst_ref=lbuf.at[c], send_sem=lsend.at[k],
            recv_sem=lrecv.at[c], device_id=(r, lax.rem(c + k, C)), device_id_type=MESH)
        copy.start()
        left_copies.append(copy)

    norm_copies = []
    for k in range(1, R):
        copy = pltpu.make_async_remote_copy(
            src_ref=norm, dst_ref=nbuf.at[r], send_sem=nsend.at[k],
            recv_sem=nrecv.at[r], device_id=(lax.rem(r + k, R), c), device_id_type=MESH)
        copy.start()
        norm_copies.append(copy)

    wcon[...] = w_con[...].astype(F32)
    wbd[...] = jnp.zeros_like(wbd)
    for d in range(F):
        block = wcon[pl.ds(d, F, stride=F), :].astype(BF16)
        for p in range(PK):
            wbd[pl.ds(d * Z + p * F, F), pl.ds(p * Z, Z)] = block

    lbuf[c] = lblk[...]
    nbuf[r] = norm[...]

    @pl.when(own_target)
    def _():
        rbuf[part, c] = rblk[...]

    zero = jnp.zeros((CH, HC), BF16)

    def doubled(m):
        return jnp.concatenate(
            [jnp.concatenate([m, zero], axis=1), jnp.concatenate([zero, m], axis=1)], axis=0)

    switch2 = doubled(switch[...])
    for s in range(S2):
        gate = jnp.dot(norm[s], switch2, preferred_element_type=F32)
        gbuf[s] = 1.0 / (1.0 + jnp.exp(-gate))

    for k in range(1, C):
        peer = lax.rem(c + k, C)
        pltpu.make_async_remote_copy(
            src_ref=lblk, dst_ref=lbuf.at[peer], send_sem=lsend.at[k],
            recv_sem=lrecv.at[peer], device_id=(r, peer), device_id_type=MESH).wait_recv()
    for half in range(HV):
        for k in range(C):
            row, col = c * HV + half, lax.rem(c + k, C)

            def arrive(half=half, row=row, col=col, k=k):
                pltpu.make_async_remote_copy(
                    src_ref=rblk, dst_ref=rbuf.at[half, col], send_sem=rsend.at[k],
                    recv_sem=rrecv.at[half, col], device_id=(row, col),
                    device_id_type=MESH).wait_recv()

            if k == 0:
                pl.when(jnp.logical_not(row == r))(arrive)
            else:
                arrive()

    count = jnp.zeros((1, 1), F32)
    for k in range(C):
        count = count + lbuf[k][S + 1:S + 2, 0:1].astype(F32)
    inv = 1.0 / count
    left = lbuf[...].reshape(C * SP, I * F)
    step = Z // I
    for half in range(HV):
        def outer(t, carry, half=half):
            at = pl.multiple_of(t * Z, Z)
            lhs = rbuf[half, :, :, pl.ds(at, Z)].reshape(C * SP, Z)
            o = lax.dot_general(lhs, left, (((0,), (0,)), ((), ())),
                                preferred_element_type=F32).astype(BF16)
            for q in range(step):
                for g in range(IG):
                    pbuf[t, pl.ds(g * J + half * I, I), pl.ds(q * Z, Z)] = (
                        o[q * I:(q + 1) * I, g * Z:(g + 1) * Z])
            return carry
        lax.fori_loop(0, F // step, outer, 0)

    ubuf[...] = jnp.zeros_like(ubuf)

    def contract(t, carry):
        at = pl.multiple_of(t * (step * Z), step * Z)
        ubuf[...] += jnp.dot(pbuf[t], wbd[pl.ds(at, step * Z), :], preferred_element_type=F32)
        return carry
    lax.fori_loop(0, F // step, contract, 0)

    rows_of, lanes_of = (lax.broadcasted_iota(jnp.int32, (I, I), n) for n in (0, 1))
    lane_parts = []
    for half in range(HV):
        lane = rbuf[half, 0][S:S + 1, 0:I].astype(F32)
        lane_parts.append(lane)
        spread = jnp.where(rows_of == lanes_of, jnp.broadcast_to(lane, (I, I)), 0.0)
        mcol[pl.ds(half * I, I), :] = jnp.broadcast_to(
            jnp.sum(spread, axis=1, keepdims=True), (I, Z))
    bias = (jnp.concatenate(lane_parts * 2, axis=1) - 1.0) * 1000000000.0

    off = offset[...]
    score_t = score[...]
    hi = I // 2
    own = lgbuf.at[c]

    def epilogue(g, carry):
        for p in range(PK):
            pieces = []
            for upper in range(2):
                i = g * PK + p + upper * hi
                row = pl.multiple_of((g + upper * (IG // 2)) * J, J)
                update = ubuf[pl.ds(row, J), p * Z:(p + 1) * Z] * inv + off
                mark = flags[i].astype(F32)
                new = (couple[i].astype(F32) + (mcol[...] * mark) * update).astype(BF16)
                pair_out[i] = new
                normed = standardize(new.astype(F32)).astype(BF16)
                pieces.append(lax.dot_general(
                    score_t, normed, (((1,), (1,)), ((), ())), preferred_element_type=F32))
            own[g * PK + p] = jnp.concatenate(pieces, axis=1) + bias
        return carry
    lax.fori_loop(0, IG // 2, epilogue, 0)

    logit_copies = []
    for k in range(1, C):
        copy = pltpu.make_async_remote_copy(
            src_ref=lgbuf.at[c], dst_ref=lgbuf.at[c], send_sem=gsend.at[k],
            recv_sem=grecv.at[c], device_id=(r, lax.rem(c + k, C)), device_id_type=MESH)
        copy.start()
        logit_copies.append(copy)

    for k in range(1, R):
        peer = lax.rem(r + k, R)
        pltpu.make_async_remote_copy(
            src_ref=norm, dst_ref=nbuf.at[peer], send_sem=nsend.at[k],
            recv_sem=nrecv.at[peer], device_id=(peer, c), device_id_type=MESH).wait_recv()
    content2 = doubled(content[...])

    def value(s, carry):
        x = nbuf[:, s].reshape(R * I, 2 * CH)
        vbuf[s] = jnp.dot(x, content2, preferred_element_type=F32).astype(BF16)
        return carry
    lax.fori_loop(0, S2, value, 0)

    for k in range(1, C):
        peer = lax.rem(c + k, C)
        pltpu.make_async_remote_copy(
            src_ref=lgbuf.at[peer], dst_ref=lgbuf.at[peer], send_sem=gsend.at[k],
            recv_sem=grecv.at[peer], device_id=(r, peer), device_id_type=MESH).wait_recv()

    for upper in range(2):
        logits = jnp.concatenate(
            [lgbuf[k].reshape(hi * H, 2 * J)[:, upper * J:(upper + 1) * J] for k in range(C)],
            axis=1)
        e = jnp.exp(logits - jnp.max(logits, axis=1, keepdims=True))
        wts = e / jnp.sum(e, axis=1, keepdims=True)
        for at in range(0, C * J, 128):
            wtmp[at // 128, pl.ds(upper * hi * H, hi * H), :] = wts[:, at:at + 128]
    weights = jnp.concatenate(
        [jnp.concatenate([wtmp[a, pl.ds(h, I, stride=H), :] for a in range(C * J // 128)], axis=1)
         for h in range(H)], axis=0).astype(BF16)

    head_lane = lax.rem(lax.broadcasted_iota(jnp.int32, (I, 2 * HC), 1), HC) // (HC // H)

    for s in range(S2):
        full = jnp.dot(weights, vbuf[s], preferred_element_type=F32)
        acc = jnp.zeros((I, 2 * HC), F32)
        for h in range(H):
            acc = jnp.where(head_lane == h, full[h * I:(h + 1) * I], acc)
        both = (gbuf[s] * acc).astype(BF16)
        gated[s] = both[:, :HC]
        gated[s + S2] = both[:, HC:]
    moved = lax.dot_general(gated[...].reshape(2 * S2 * I, HC), final[...],
                            (((1,), (1,)), ((), ())), preferred_element_type=F32)
    hom_out[...] = (hom[...].astype(F32)
                    + moved.reshape(2 * S2, I, CH)[:S]).astype(BF16)

    for k in range(1, R):
        right_copy(k, lax.rem(r + k, R)).wait_send()

    @pl.when(jnp.logical_not(own_target))
    def _():
        right_copy(0, r).wait_send()
    for copy in left_copies + norm_copies + logit_copies:
        copy.wait_send()


def solution(mesh):
    R, C = mesh.shape["row"], mesh.shape["col"]

    def body(couple, hom, flags, avail, w_left, w_right, w_con, offset, score, content, switch,
             final):
        S, I, CH = hom.shape
        J, Z = couple.shape[1:]
        F = w_left.shape[1]
        H = score.shape[1]
        HC = content.shape[1]
        S2 = (S + 1) // 2
        SP = -(-(S + 2) // 16) * 16
        step = Z // I
        vmem = pl.BlockSpec(memory_space=pltpu.VMEM)
        smem = pl.BlockSpec(memory_space=pltpu.SMEM)
        dma = pltpu.SemaphoreType.DMA
        return pl.pallas_call(
            functools.partial(kernel, R, C, S),
            out_shape=(jax.ShapeDtypeStruct(couple.shape, BF16),
                       jax.ShapeDtypeStruct(hom.shape, BF16)),
            in_specs=[vmem, vmem, smem, vmem, smem] + [vmem] * 8,
            out_specs=(vmem, vmem),
            scratch_shapes=[
                pltpu.VMEM((S2, I, 2 * CH), BF16),
                pltpu.VMEM((SP, I * F), BF16),
                pltpu.VMEM((SP, F * I), BF16),
                pltpu.VMEM((F * F, Z), F32),
                pltpu.VMEM((2 * S2, I, HC), BF16),
                pltpu.VMEM((C, SP, I * F), BF16),
                pltpu.VMEM((J // I, C, SP, F * I), BF16),
                pltpu.VMEM((R, S2, I, 2 * CH), BF16),
                pltpu.VMEM((C, I // 2, H, 2 * J), F32),
                pltpu.VMEM((F * Z, Z // F * Z), BF16),
                pltpu.VMEM((F // step, I * F // Z * J, step * Z), BF16),
                pltpu.VMEM((I * F // Z * J, Z // F * Z), F32),
                pltpu.VMEM((S2, R * I, 2 * HC), BF16),
                pltpu.VMEM((S2, I, 2 * HC), F32),
                pltpu.VMEM((C * J // 128, I * H, 128), F32),
                pltpu.VMEM((J, Z), F32),
                dma((C,)), dma((C,)), dma((R,)), dma((J // I, C)),
                dma((R,)), dma((R,)), dma((C,)), dma((C,)),
            ],
            compiler_params=pltpu.CompilerParams(
                collective_id=0, has_side_effects=True, vmem_limit_bytes=56 * 2**20),
        )(couple, hom, flags, flags.reshape(1, I), avail, w_left.T, w_right.T, w_con,
          offset.reshape(1, Z), score.T, content, switch, final.T)

    placed = (P("row", "col", None), P("col", "row", None), P("row"), P("col")) + (P(),) * 8
    return jax.shard_map(
        body, mesh=mesh, in_specs=placed,
        out_specs=(P("row", "col", None), P("col", "row", None)), check_vma=False)
```

```python
import functools

import jax
import jax.numpy as jnp
from jax import lax
from jax.experimental import pallas as pl
from jax.experimental.pallas import tpu as pltpu
from jax.sharding import PartitionSpec as P

EPSILON = 1e-05
MESH = pl.DeviceIdType.MESH
BF16 = jnp.bfloat16
F32 = jnp.float32


def standardize(inputs):
    mean_value = jnp.mean(inputs, axis=-1, keepdims=True)
    centered = inputs - mean_value
    variance = jnp.mean(centered * centered, axis=-1, keepdims=True)
    return centered * lax.rsqrt(variance + EPSILON)


def kernel(
    R, C, S,
    couple, hom, flags, flag_row, avail, w_left, w_right, w_con, offset, score, content, switch,
    final, pair_out, hom_out,
    norm, lblk, rblk, wcon, gated, lbuf, rbuf, nbuf, lgbuf, wbd, pbuf, ubuf, vbuf, gbuf, wtmp, mcol,
    lsend, lrecv, rsend, rrecv, nsend, nrecv, gsend, grecv,
):
    I, J, Z = couple.shape
    F = w_left.shape[0]
    H = score.shape[0]
    S2 = norm.shape[0]
    CH = norm.shape[2] // 2
    HC = content.shape[1]
    HV = J // I
    SP = lblk.shape[0]
    PK = Z // F
    IG = I // PK
    r = lax.axis_index("row")
    c = lax.axis_index("col")
    target = lax.div(r, HV)
    part = lax.rem(r, HV)
    own_target = target == c

    barrier = pltpu.get_barrier_semaphore()

    def greet(row, col):
        pl.semaphore_signal(barrier, inc=1, device_id=(row, col), device_id_type=MESH)

    for k in range(1, C):
        greet(r, lax.rem(c + k, C))
    for k in range(1, R):
        greet(lax.rem(r + k, R), c)
    for half in range(HV):
        for k in range(C):
            row, col = c * HV + half, lax.rem(c + k, C)
            if k == 0:
                pl.when(jnp.logical_not(row == r))(functools.partial(greet, row, col))
            else:
                greet(row, col)

    normed = standardize(hom[...].reshape(S * I, CH).astype(F32)).astype(BF16)
    if S % 2:
        padded = jnp.concatenate([normed, jnp.zeros((I, CH), BF16)], axis=0)
    else:
        padded = normed
    norm[...] = jnp.concatenate(
        [padded[:S2 * I], padded[S2 * I:]], axis=1).reshape(S2, I, 2 * CH)
    feat, lane = (lax.broadcasted_iota(jnp.int32, (F, I * F), n) for n in (0, 1))
    low_f = (lax.rem(lane, F) == feat).astype(F32).astype(BF16)
    high_f = (lax.div(lane, I) == feat).astype(F32).astype(BF16)
    res, lane = (lax.broadcasted_iota(jnp.int32, (I, I * F), n) for n in (0, 1))
    high_i = (lax.div(lane, F) == res).astype(F32)
    low_i = (lax.rem(lane, I) == res).astype(F32)
    seq, lane = (lax.broadcasted_iota(jnp.int32, (SP, S * I), n) for n in (0, 1))
    mark = jnp.zeros((SP, S * I), F32)
    count = jnp.int32(0)
    for n in range(S):
        mark = jnp.where(seq == n, avail[n].astype(F32), mark)
        count = count + avail[n]
    pick = jnp.where(lax.div(lane, I) == seq, mark, 0.0).astype(BF16)
    rows = lax.broadcasted_iota(jnp.int32, (SP, I * F), 0)

    def factors(weight, spread, keep):
        wide = lax.dot_general(weight[...], spread, (((0,), (0,)), ((), ())),
                               preferred_element_type=F32).astype(BF16)
        every = jnp.dot(normed, wide, preferred_element_type=F32).reshape(S, I, I * F)
        own = (every * keep[None]).astype(BF16).reshape(S * I, I * F)
        return jnp.dot(pick, own, preferred_element_type=F32)

    right = factors(w_right, high_f, low_i)
    tok = jnp.dot(jnp.broadcast_to(flag_row[...].astype(F32), (SP, I)).astype(BF16),
                  low_i.astype(BF16), preferred_element_type=F32)
    rblk[...] = jnp.where(rows == S, tok, right).astype(BF16)
    left = factors(w_left, low_f, high_i)
    lblk[...] = jnp.where(rows == S + 1, count.astype(F32), left).astype(BF16)

    pl.semaphore_wait(barrier, (C - 1) + (R - 1) + R - own_target.astype(jnp.int32))

    def right_copy(k, row):
        return pltpu.make_async_remote_copy(
            src_ref=rblk, dst_ref=rbuf.at[part, c], send_sem=rsend.at[k],
            recv_sem=rrecv.at[part, c], device_id=(row, target), device_id_type=MESH)

    for k in range(1, R):
        right_copy(k, lax.rem(r + k, R)).start()

    @pl.when(jnp.logical_not(own_target))
    def _():
        right_copy(0, r).start()

    left_copies = []
    for k in range(1, C):
        copy = pltpu.make_async_remote_copy(
            src_ref=lblk, dst_ref=lbuf.at[c], send_sem=lsend.at[k],
            recv_sem=lrecv.at[c], device_id=(r, lax.rem(c + k, C)), device_id_type=MESH)
        copy.start()
        left_copies.append(copy)

    wcon[...] = w_con[...].astype(F32)
    wbd[...] = jnp.zeros_like(wbd)
    for d in range(F):
        block = wcon[pl.ds(d, F, stride=F), :].astype(BF16)
        for p in range(PK):
            wbd[pl.ds(d * Z + p * F, F), pl.ds(p * Z, Z)] = block

    lbuf[c] = lblk[...]
    nbuf[r] = norm[...]

    @pl.when(own_target)
    def _():
        rbuf[part, c] = rblk[...]

    zero = jnp.zeros((CH, HC), BF16)

    def doubled(m):
        return jnp.concatenate(
            [jnp.concatenate([m, zero], axis=1), jnp.concatenate([zero, m], axis=1)], axis=0)

    switch2 = doubled(switch[...])
    for s in range(S2):
        gate = jnp.dot(norm[s], switch2, preferred_element_type=F32)
        gbuf[s] = 1.0 / (1.0 + jnp.exp(-gate))

    for k in range(1, C):
        peer = lax.rem(c + k, C)
        pltpu.make_async_remote_copy(
            src_ref=lblk, dst_ref=lbuf.at[peer], send_sem=lsend.at[k],
            recv_sem=lrecv.at[peer], device_id=(r, peer), device_id_type=MESH).wait_recv()
    for half in range(HV):
        for k in range(C):
            row, col = c * HV + half, lax.rem(c + k, C)

            def arrive(half=half, row=row, col=col, k=k):
                pltpu.make_async_remote_copy(
                    src_ref=rblk, dst_ref=rbuf.at[half, col], send_sem=rsend.at[k],
                    recv_sem=rrecv.at[half, col], device_id=(row, col),
                    device_id_type=MESH).wait_recv()

            if k == 0:
                pl.when(jnp.logical_not(row == r))(arrive)
            else:
                arrive()

    norm_copies = []
    for k in range(1, R):
        copy = pltpu.make_async_remote_copy(
            src_ref=norm, dst_ref=nbuf.at[r], send_sem=nsend.at[k],
            recv_sem=nrecv.at[r], device_id=(lax.rem(r + k, R), c), device_id_type=MESH)
        copy.start()
        norm_copies.append(copy)

    count = jnp.zeros((1, 1), F32)
    for k in range(C):
        count = count + lbuf[k][S + 1:S + 2, 0:1].astype(F32)
    inv = 1.0 / count
    left = lbuf[...].reshape(C * SP, I * F)
    wide = min(256, F * I)
    for half in range(HV):
        def outer(t, carry, half=half):
            at = pl.multiple_of(t * wide, wide)
            lhs = rbuf[half, :, :, pl.ds(at, wide)].reshape(C * SP, wide)
            o = lax.dot_general(lhs, left, (((0,), (0,)), ((), ())),
                                preferred_element_type=F32).astype(BF16)
            for q in range(wide // I):
                to = pl.multiple_of(t * (wide // I * Z) + q * Z, Z)
                for g in range(IG):
                    pbuf[pl.ds(g * J + half * I, I), pl.ds(to, Z)] = (
                        o[q * I:(q + 1) * I, g * Z:(g + 1) * Z])
            return carry
        lax.fori_loop(0, F * I // wide, outer, 0)

    tall = min(256, IG * J)

    def contract(t, carry):
        at = pl.multiple_of(t * tall, tall)
        ubuf[pl.ds(at, tall), :] = jnp.dot(
            pbuf[pl.ds(at, tall), :], wbd[...], preferred_element_type=F32)
        return carry
    lax.fori_loop(0, IG * J // tall, contract, 0)

    rows_of, lanes_of = (lax.broadcasted_iota(jnp.int32, (I, I), n) for n in (0, 1))
    lane_parts = []
    for half in range(HV):
        lane = rbuf[half, 0][S:S + 1, 0:I].astype(F32)
        lane_parts.append(lane)
        spread = jnp.where(rows_of == lanes_of, jnp.broadcast_to(lane, (I, I)), 0.0)
        mcol[pl.ds(half * I, I), :] = jnp.broadcast_to(
            jnp.sum(spread, axis=1, keepdims=True), (I, Z))
    bias = (jnp.concatenate(lane_parts * 2, axis=1) - 1.0) * 1000000000.0

    off = offset[...]
    score_t = score[...]
    hi = I // 2
    own = lgbuf.at[c]

    def logit_copy(slot, g, k):
        piece = lgbuf.at[slot, pl.ds(g * PK, PK)]
        return pltpu.make_async_remote_copy(
            src_ref=piece, dst_ref=piece, send_sem=gsend.at[k, g],
            recv_sem=grecv.at[slot, g], device_id=(r, lax.rem(c + k, C)), device_id_type=MESH)

    def epilogue(g, carry):
        for p in range(PK):
            pieces = []
            for upper in range(2):
                i = g * PK + p + upper * hi
                row = pl.multiple_of((g + upper * (IG // 2)) * J, J)
                update = ubuf[pl.ds(row, J), p * Z:(p + 1) * Z] * inv + off
                mark = flags[i].astype(F32)
                new = (couple[i].astype(F32) + (mcol[...] * mark) * update).astype(BF16)
                pair_out[i] = new
                normed = standardize(new.astype(F32)).astype(BF16)
                pieces.append(lax.dot_general(
                    score_t, normed, (((1,), (1,)), ((), ())), preferred_element_type=F32))
            own[g * PK + p] = jnp.concatenate(pieces, axis=1) + bias
        for k in range(1, C):
            logit_copy(c, g, k).start()
        return carry
    lax.fori_loop(0, IG // 2, epilogue, 0)

    for k in range(1, R):
        peer = lax.rem(r + k, R)
        pltpu.make_async_remote_copy(
            src_ref=norm, dst_ref=nbuf.at[peer], send_sem=nsend.at[k],
            recv_sem=nrecv.at[peer], device_id=(peer, c), device_id_type=MESH).wait_recv()
    content2 = doubled(content[...])

    def value(s, carry):
        x = nbuf[:, s].reshape(R * I, 2 * CH)
        vbuf[s] = jnp.dot(x, content2, preferred_element_type=F32).astype(BF16)
        return carry
    lax.fori_loop(0, S2, value, 0)

    for k in range(1, C):
        for g in range(IG // 2):
            logit_copy(lax.rem(c + k, C), g, k).wait_recv()

    for upper in range(2):
        logits = jnp.concatenate(
            [lgbuf[k].reshape(hi * H, 2 * J)[:, upper * J:(upper + 1) * J] for k in range(C)],
            axis=1)
        e = jnp.exp(logits - jnp.max(logits, axis=1, keepdims=True))
        wts = e / jnp.sum(e, axis=1, keepdims=True)
        for at in range(0, C * J, 128):
            wtmp[at // 128, pl.ds(upper * hi * H, hi * H), :] = wts[:, at:at + 128]
    weights = jnp.concatenate(
        [jnp.concatenate([wtmp[a, pl.ds(h, I, stride=H), :] for a in range(C * J // 128)], axis=1)
         for h in range(H)], axis=0).astype(BF16)

    head_lane = lax.rem(lax.broadcasted_iota(jnp.int32, (I, 2 * HC), 1), HC) // (HC // H)

    for s in range(S2):
        full = jnp.dot(weights, vbuf[s], preferred_element_type=F32)
        acc = jnp.zeros((I, 2 * HC), F32)
        for h in range(H):
            acc = jnp.where(head_lane == h, full[h * I:(h + 1) * I], acc)
        both = (gbuf[s] * acc).astype(BF16)
        gated[s] = both[:, :HC]
        gated[s + S2] = both[:, HC:]
    moved = lax.dot_general(gated[...].reshape(2 * S2 * I, HC), final[...],
                            (((1,), (1,)), ((), ())), preferred_element_type=F32)
    hom_out[...] = (hom[...].astype(F32)
                    + moved.reshape(2 * S2, I, CH)[:S]).astype(BF16)

    for k in range(1, R):
        right_copy(k, lax.rem(r + k, R)).wait_send()

    @pl.when(jnp.logical_not(own_target))
    def _():
        right_copy(0, r).wait_send()
    for copy in left_copies + norm_copies:
        copy.wait_send()
    for k in range(1, C):
        for g in range(IG // 2):
            logit_copy(c, g, k).wait_send()


def solution(mesh):
    R, C = mesh.shape["row"], mesh.shape["col"]

    def body(couple, hom, flags, avail, w_left, w_right, w_con, offset, score, content, switch,
             final):
        S, I, CH = hom.shape
        J, Z = couple.shape[1:]
        F = w_left.shape[1]
        H = score.shape[1]
        HC = content.shape[1]
        S2 = (S + 1) // 2
        SP = -(-(S + 2) // 16) * 16
        vmem = pl.BlockSpec(memory_space=pltpu.VMEM)
        smem = pl.BlockSpec(memory_space=pltpu.SMEM)
        dma = pltpu.SemaphoreType.DMA
        return pl.pallas_call(
            functools.partial(kernel, R, C, S),
            out_shape=(jax.ShapeDtypeStruct(couple.shape, BF16),
                       jax.ShapeDtypeStruct(hom.shape, BF16)),
            in_specs=[vmem, vmem, smem, vmem, smem] + [vmem] * 8,
            out_specs=(vmem, vmem),
            scratch_shapes=[
                pltpu.VMEM((S2, I, 2 * CH), BF16),
                pltpu.VMEM((SP, I * F), BF16),
                pltpu.VMEM((SP, F * I), BF16),
                pltpu.VMEM((F * F, Z), F32),
                pltpu.VMEM((2 * S2, I, HC), BF16),
                pltpu.VMEM((C, SP, I * F), BF16),
                pltpu.VMEM((J // I, C, SP, F * I), BF16),
                pltpu.VMEM((R, S2, I, 2 * CH), BF16),
                pltpu.VMEM((C, I // 2, H, 2 * J), F32),
                pltpu.VMEM((F * Z, Z // F * Z), BF16),
                pltpu.VMEM((I * F // Z * J, F * Z), BF16),
                pltpu.VMEM((I * F // Z * J, Z // F * Z), F32),
                pltpu.VMEM((S2, R * I, 2 * HC), BF16),
                pltpu.VMEM((S2, I, 2 * HC), F32),
                pltpu.VMEM((C * J // 128, I * H, 128), F32),
                pltpu.VMEM((J, Z), F32),
                dma((C,)), dma((C,)), dma((R,)), dma((J // I, C)),
                dma((R,)), dma((R,)), dma((C, I * F // Z // 2)), dma((C, I * F // Z // 2)),
            ],
            compiler_params=pltpu.CompilerParams(
                collective_id=0, has_side_effects=True, vmem_limit_bytes=56 * 2**20),
        )(couple, hom, flags, flags.reshape(1, I), avail, w_left.T, w_right.T, w_con,
          offset.reshape(1, Z), score.T, content, switch, final.T)

    placed = (P("row", "col", None), P("col", "row", None), P("row"), P("col")) + (P(),) * 8
    return jax.shard_map(
        body, mesh=mesh, in_specs=placed,
        out_specs=(P("row", "col", None), P("col", "row", None)), check_vma=False)
```

```python
import functools

import jax
import jax.numpy as jnp
from jax import lax
from jax.experimental import pallas as pl
from jax.experimental.pallas import tpu as pltpu
from jax.sharding import PartitionSpec as P

EPSILON = 1e-05
MESH = pl.DeviceIdType.MESH
BF16 = jnp.bfloat16
F32 = jnp.float32


def standardize(inputs):
    mean_value = jnp.mean(inputs, axis=-1, keepdims=True)
    centered = inputs - mean_value
    variance = jnp.mean(centered * centered, axis=-1, keepdims=True)
    return centered * lax.rsqrt(variance + EPSILON)


def kernel(
    R, C, S,
    couple, hom, flags, flag_row, avail, w_left, w_right, w_con, offset, score, content, switch,
    final, pair_out, hom_out,
    norm, lblk, rblk, wcon, gated, lbuf, rbuf, nbuf, lgbuf, wbd, pbuf, ubuf, vbuf, gbuf, wtmp, mcol,
    lsend, lrecv, rsend, rrecv, nsend, nrecv, gsend, grecv,
):
    I, J, Z = couple.shape
    F = w_left.shape[0]
    H = score.shape[0]
    S2 = norm.shape[0]
    CH = norm.shape[2] // 2
    HC = content.shape[1]
    HV = J // I
    SP = lblk.shape[0]
    PK = Z // F
    IG = I // PK
    r = lax.axis_index("row")
    c = lax.axis_index("col")
    target = lax.div(r, HV)
    part = lax.rem(r, HV)
    own_target = target == c

    barrier = pltpu.get_barrier_semaphore()

    def greet(row, col):
        pl.semaphore_signal(barrier, inc=1, device_id=(row, col), device_id_type=MESH)

    for k in range(1, C):
        greet(r, lax.rem(c + k, C))
    for k in range(1, R):
        greet(lax.rem(r + k, R), c)
    for half in range(HV):
        for k in range(C):
            row, col = c * HV + half, lax.rem(c + k, C)
            if k == 0:
                pl.when(jnp.logical_not(row == r))(functools.partial(greet, row, col))
            else:
                greet(row, col)

    normed = standardize(hom[...].reshape(S * I, CH).astype(F32)).astype(BF16)
    if S % 2:
        padded = jnp.concatenate([normed, jnp.zeros((I, CH), BF16)], axis=0)
    else:
        padded = normed
    norm[...] = jnp.concatenate(
        [padded[:S2 * I], padded[S2 * I:]], axis=1).reshape(S2, I, 2 * CH)
    feat, lane = (lax.broadcasted_iota(jnp.int32, (F, I * F), n) for n in (0, 1))
    low_f = (lax.rem(lane, F) == feat).astype(F32).astype(BF16)
    high_f = (lax.div(lane, I) == feat).astype(F32).astype(BF16)
    res, lane = (lax.broadcasted_iota(jnp.int32, (I, I * F), n) for n in (0, 1))
    high_i = (lax.div(lane, F) == res).astype(F32)
    low_i = (lax.rem(lane, I) == res).astype(F32)
    seq, lane = (lax.broadcasted_iota(jnp.int32, (SP, S * I), n) for n in (0, 1))
    mark = jnp.zeros((SP, S * I), F32)
    count = jnp.int32(0)
    for n in range(S):
        mark = jnp.where(seq == n, avail[n].astype(F32), mark)
        count = count + avail[n]
    pick = jnp.where(lax.div(lane, I) == seq, mark, 0.0).astype(BF16)
    rows = lax.broadcasted_iota(jnp.int32, (SP, I * F), 0)

    def factors(weight, spread, keep):
        wide = lax.dot_general(weight[...], spread, (((0,), (0,)), ((), ())),
                               preferred_element_type=F32).astype(BF16)
        every = jnp.dot(normed, wide, preferred_element_type=F32).reshape(S, I, I * F)
        own = (every * keep[None]).astype(BF16).reshape(S * I, I * F)
        return jnp.dot(pick, own, preferred_element_type=F32)

    right = factors(w_right, high_f, low_i)
    tok = jnp.dot(jnp.broadcast_to(flag_row[...].astype(F32), (SP, I)).astype(BF16),
                  low_i.astype(BF16), preferred_element_type=F32)
    rblk[...] = jnp.where(rows == S, tok, right).astype(BF16)
    left = factors(w_left, low_f, high_i)
    lblk[...] = jnp.where(rows == S + 1, count.astype(F32), left).astype(BF16)

    pl.semaphore_wait(barrier, (C - 1) + (R - 1) + R - own_target.astype(jnp.int32))

    def right_copy(k, row):
        return pltpu.make_async_remote_copy(
            src_ref=rblk, dst_ref=rbuf.at[part, c], send_sem=rsend.at[k],
            recv_sem=rrecv.at[part, c], device_id=(row, target), device_id_type=MESH)

    for k in range(1, R):
        right_copy(k, lax.rem(r + k, R)).start()

    @pl.when(jnp.logical_not(own_target))
    def _():
        right_copy(0, r).start()

    left_copies = []
    for k in range(1, C):
        copy = pltpu.make_async_remote_copy(
            src_ref=lblk, dst_ref=lbuf.at[c], send_sem=lsend.at[k],
            recv_sem=lrecv.at[c], device_id=(r, lax.rem(c + k, C)), device_id_type=MESH)
        copy.start()
        left_copies.append(copy)

    wcon[...] = w_con[...].astype(F32)
    wbd[...] = jnp.zeros_like(wbd)
    for d in range(F):
        block = wcon[pl.ds(d, F, stride=F), :].astype(BF16)
        for p in range(PK):
            wbd[pl.ds(d * Z + p * F, F), pl.ds(p * Z, Z)] = block

    lbuf[c] = lblk[...]
    nbuf[r] = norm[...]

    @pl.when(own_target)
    def _():
        rbuf[part, c] = rblk[...]

    zero = jnp.zeros((CH, HC), BF16)

    def doubled(m):
        return jnp.concatenate(
            [jnp.concatenate([m, zero], axis=1), jnp.concatenate([zero, m], axis=1)], axis=0)

    switch2 = doubled(switch[...])
    for s in range(S2):
        gate = jnp.dot(norm[s], switch2, preferred_element_type=F32)
        gbuf[s] = 1.0 / (1.0 + jnp.exp(-gate))

    for k in range(1, C):
        peer = lax.rem(c + k, C)
        pltpu.make_async_remote_copy(
            src_ref=lblk, dst_ref=lbuf.at[peer], send_sem=lsend.at[k],
            recv_sem=lrecv.at[peer], device_id=(r, peer), device_id_type=MESH).wait_recv()
    for half in range(HV):
        for k in range(C):
            row, col = c * HV + half, lax.rem(c + k, C)

            def arrive(half=half, row=row, col=col, k=k):
                pltpu.make_async_remote_copy(
                    src_ref=rblk, dst_ref=rbuf.at[half, col], send_sem=rsend.at[k],
                    recv_sem=rrecv.at[half, col], device_id=(row, col),
                    device_id_type=MESH).wait_recv()

            if k == 0:
                pl.when(jnp.logical_not(row == r))(arrive)
            else:
                arrive()

    norm_copies = []
    for k in range(1, R):
        copy = pltpu.make_async_remote_copy(
            src_ref=norm, dst_ref=nbuf.at[r], send_sem=nsend.at[k],
            recv_sem=nrecv.at[r], device_id=(lax.rem(r + k, R), c), device_id_type=MESH)
        copy.start()
        norm_copies.append(copy)

    count = jnp.zeros((1, 1), F32)
    for k in range(C):
        count = count + lbuf[k][S + 1:S + 2, 0:1].astype(F32)
    inv = 1.0 / count
    left = lbuf[...].reshape(C * SP, I * F)
    wide = min(256, F * I)
    for half in range(HV):
        def outer(t, carry, half=half):
            at = pl.multiple_of(t * wide, wide)
            lhs = rbuf[half, :, :, pl.ds(at, wide)].reshape(C * SP, wide)
            o = lax.dot_general(lhs, left, (((0,), (0,)), ((), ())),
                                preferred_element_type=F32).astype(BF16)
            for q in range(wide // I):
                to = pl.multiple_of(t * (wide // I * Z) + q * Z, Z)
                for g in range(IG):
                    pbuf[pl.ds(g * J + half * I, I), pl.ds(to, Z)] = (
                        o[q * I:(q + 1) * I, g * Z:(g + 1) * Z])
            return carry
        lax.fori_loop(0, F * I // wide, outer, 0)

    tall = min(256, IG * J)

    def contract(t, carry):
        at = pl.multiple_of(t * tall, tall)
        ubuf[pl.ds(at, tall), :] = jnp.dot(
            pbuf[pl.ds(at, tall), :], wbd[...], preferred_element_type=F32)
        return carry
    lax.fori_loop(0, IG * J // tall, contract, 0)

    rows_of, lanes_of = (lax.broadcasted_iota(jnp.int32, (I, I), n) for n in (0, 1))
    lane_parts = []
    for half in range(HV):
        lane = rbuf[half, 0][S:S + 1, 0:I].astype(F32)
        lane_parts.append(lane)
        spread = jnp.where(rows_of == lanes_of, jnp.broadcast_to(lane, (I, I)), 0.0)
        mcol[pl.ds(half * I, I), :] = jnp.broadcast_to(
            jnp.sum(spread, axis=1, keepdims=True), (I, Z))
    bias = (jnp.concatenate(lane_parts * 2, axis=1) - 1.0) * 1000000000.0

    off = offset[...]
    score_t = score[...]
    hi = I // 2
    own = lgbuf.at[c]

    def logit_copy(slot, g, k):
        piece = lgbuf.at[slot, pl.ds(g * PK, PK)]
        return pltpu.make_async_remote_copy(
            src_ref=piece, dst_ref=piece, send_sem=gsend.at[k, g],
            recv_sem=grecv.at[slot, g], device_id=(r, lax.rem(c + k, C)), device_id_type=MESH)

    def epilogue(g, carry):
        for p in range(PK):
            pieces = []
            for upper in range(2):
                i = g * PK + p + upper * hi
                row = pl.multiple_of((g + upper * (IG // 2)) * J, J)
                update = ubuf[pl.ds(row, J), p * Z:(p + 1) * Z] * inv + off
                mark = flags[i].astype(F32)
                new = (couple[i].astype(F32) + (mcol[...] * mark) * update).astype(BF16)
                pair_out[i] = new
                normed = standardize(new.astype(F32)).astype(BF16)
                pieces.append(lax.dot_general(
                    score_t, normed, (((1,), (1,)), ((), ())), preferred_element_type=F32))
            own[g * PK + p] = jnp.concatenate(pieces, axis=1) + bias
        for k in range(1, C):
            logit_copy(c, g, k).start()
        return carry
    lax.fori_loop(0, IG // 2, epilogue, 0)

    for k in range(1, R):
        peer = lax.rem(r + k, R)
        pltpu.make_async_remote_copy(
            src_ref=norm, dst_ref=nbuf.at[peer], send_sem=nsend.at[k],
            recv_sem=nrecv.at[peer], device_id=(peer, c), device_id_type=MESH).wait_recv()
    content2 = doubled(content[...])

    def value(s, carry):
        x = nbuf[:, s].reshape(R * I, 2 * CH)
        vbuf[s] = jnp.dot(x, content2, preferred_element_type=F32).astype(BF16)
        return carry
    lax.fori_loop(0, S2, value, 0)

    for k in range(1, C):
        for g in range(IG // 2):
            logit_copy(lax.rem(c + k, C), g, k).wait_recv()

    for upper in range(2):
        logits = jnp.concatenate(
            [lgbuf[k].reshape(hi * H, 2 * J)[:, upper * J:(upper + 1) * J] for k in range(C)],
            axis=1)
        e = jnp.exp(logits - jnp.max(logits, axis=1, keepdims=True))
        wts = e / jnp.sum(e, axis=1, keepdims=True)
        for at in range(0, C * J, 128):
            wtmp[at // 128, pl.ds(upper * hi * H, hi * H), :] = wts[:, at:at + 128]
    weights = jnp.concatenate(
        [jnp.concatenate([wtmp[a, pl.ds(h, I, stride=H), :] for a in range(C * J // 128)], axis=1)
         for h in range(H)], axis=0).astype(BF16)

    head_lane = lax.rem(lax.broadcasted_iota(jnp.int32, (I, 2 * HC), 1), HC) // (HC // H)

    for s in range(S2):
        full = jnp.dot(weights, vbuf[s], preferred_element_type=F32)
        acc = jnp.zeros((I, 2 * HC), F32)
        for h in range(H):
            acc = jnp.where(head_lane == h, full[h * I:(h + 1) * I], acc)
        both = (gbuf[s] * acc).astype(BF16)
        gated[s] = both[:, :HC]
        gated[s + S2] = both[:, HC:]
    moved = lax.dot_general(gated[...].reshape(2 * S2 * I, HC), final[...],
                            (((1,), (1,)), ((), ())), preferred_element_type=F32)
    hom_out[...] = (hom[...].astype(F32)
                    + moved.reshape(2 * S2, I, CH)[:S]).astype(BF16)

    for k in range(1, R):
        right_copy(k, lax.rem(r + k, R)).wait_send()

    @pl.when(jnp.logical_not(own_target))
    def _():
        right_copy(0, r).wait_send()
    for copy in left_copies + norm_copies:
        copy.wait_send()
    for k in range(1, C):
        for g in range(IG // 2):
            logit_copy(c, g, k).wait_send()


def solution(mesh):
    R, C = mesh.shape["row"], mesh.shape["col"]

    def body(couple, hom, flags, avail, w_left, w_right, w_con, offset, score, content, switch,
             final):
        S, I, CH = hom.shape
        J, Z = couple.shape[1:]
        F = w_left.shape[1]
        H = score.shape[1]
        HC = content.shape[1]
        S2 = (S + 1) // 2
        SP = -(-(S + 2) // 16) * 16
        vmem = pl.BlockSpec(memory_space=pltpu.VMEM)
        smem = pl.BlockSpec(memory_space=pltpu.SMEM)
        dma = pltpu.SemaphoreType.DMA
        return pl.pallas_call(
            functools.partial(kernel, R, C, S),
            out_shape=(pltpu.VMEM(couple.shape, BF16), pltpu.VMEM(hom.shape, BF16)),
            in_specs=[vmem, vmem, smem, vmem, smem] + [vmem] * 8,
            out_specs=(vmem, vmem),
            scratch_shapes=[
                pltpu.VMEM((S2, I, 2 * CH), BF16),
                pltpu.VMEM((SP, I * F), BF16),
                pltpu.VMEM((SP, F * I), BF16),
                pltpu.VMEM((F * F, Z), F32),
                pltpu.VMEM((2 * S2, I, HC), BF16),
                pltpu.VMEM((C, SP, I * F), BF16),
                pltpu.VMEM((J // I, C, SP, F * I), BF16),
                pltpu.VMEM((R, S2, I, 2 * CH), BF16),
                pltpu.VMEM((C, I // 2, H, 2 * J), F32),
                pltpu.VMEM((F * Z, Z // F * Z), BF16),
                pltpu.VMEM((I * F // Z * J, F * Z), BF16),
                pltpu.VMEM((I * F // Z * J, Z // F * Z), F32),
                pltpu.VMEM((S2, R * I, 2 * HC), BF16),
                pltpu.VMEM((S2, I, 2 * HC), F32),
                pltpu.VMEM((C * J // 128, I * H, 128), F32),
                pltpu.VMEM((J, Z), F32),
                dma((C,)), dma((C,)), dma((R,)), dma((J // I, C)),
                dma((R,)), dma((R,)), dma((C, I * F // Z // 2)), dma((C, I * F // Z // 2)),
            ],
            compiler_params=pltpu.CompilerParams(
                collective_id=0, has_side_effects=True, vmem_limit_bytes=56 * 2**20),
        )(couple, hom, flags, flags.reshape(1, I), avail, w_left.T, w_right.T, w_con,
          offset.reshape(1, Z), score.T, content, switch, final.T)

    placed = (P("row", "col", None), P("col", "row", None), P("row"), P("col")) + (P(),) * 8
    return jax.shard_map(
        body, mesh=mesh, in_specs=placed,
        out_specs=(P("row", "col", None), P("col", "row", None)), check_vma=False)
```
